32 devices in a mesh: grp: 2 (over x), row: 16 (over z, y, core).
Axes of the slice: x: 2, y: 2, z: 4, core: 2. Of those that a mesh axis runs over, the one named last changes fastest.
Arguments:
- tokens: bfloat16 [512, 8192], P(('grp', 'row')), parts along dimension 0, may hold values from -6 to 6
- attention_norm_gain: float32 [8192], replicated, may hold values from 0.1 to 1.9
- query_weight: bfloat16 [8192, 8192], P(None, 'row'), may hold values from -0.0625 to 0.0625
- keyvalue_weight: bfloat16 [8192, 2, 1024], P(None, None, 'row'), may hold values from -0.0625 to 0.0625
- adapter_down_weight: bfloat16 [64, 64, 8192], P('row'), may hold values from -0.0625 to 0.0625
- adapter_query_up: bfloat16 [64, 32, 8192], P(None, None, 'row'), may hold values from -1 to 1
- adapter_value_up: bfloat16 [64, 32, 1024], P(None, None, 'row'), may hold values from -1 to 1
- cached_rotated_keys: bfloat16 [512, 48, 1024], P(('grp', 'row')), parts along dimension 0, may hold values from -102 to 102
- cached_value_rows: bfloat16 [512, 48, 1024], P(('grp', 'row')), parts along dimension 0, may hold values from -6 to 6
- row_adapter_index: int32 [512], P('grp'), parts along dimension 0, may hold values from 0 to 63, as said below
Outputs:
- context: bfloat16 [512, 8192], P(('grp', 'row')), parts along dimension 0
- new_keys: bfloat16 [512, 1024], P(('grp', 'row')), parts along dimension 0
- incoming_values: bfloat16 [512, 1024], P(('grp', 'row')), parts along dimension 0
The draws below stay inside these ranges and needn't reach their ends.
There are 2 independent parts, one for each index of `grp`. The reference program is written for one: setup_inputs(seed, part) draws one part's arguments, and reference() takes and returns one part's arrays. A program takes and returns all parts, laid end to end along the dimension named above; an argument that names none is the same for every part. Nothing has to cross between parts.
Inputs may be any that keep to these rules, and one draw needn't show every extreme that they name: `row_adapter_index`: the adapter a is owned by index a // 4 of row; no index owns the adapters of more than 64 rows, and 16 / 8 indices (two here, eight on the larger slice) own exactly 64.
All inputs are finite; a program needn't handle non-finite values.
Results may differ from the reference program's by a relative error of at most 0.009.
The reference program's roundings to bfloat16 on the way count: a program that leaves them out, or rounds other values in their place, can miss the bound.
Values may be sent and summed in bfloat16 or wider, within the bound.
A program may use at most 128 MiB of HBM per device.

```python
import math
import jax
import jax.numpy as jnp
from jax import lax

MODEL_DIMENSION = 8192
HEADS = 64
KV_HEADS = 8
HEAD_DIM = 128
ADAPTER_RANK = 32
ADP_DEV = 4
ROW_DEV = 16
PREFIX = 48
KEYVALUE_WIDTH = 1024
ROWS = 256
ADAPTER_COUNT = 64
CAPO = 64
N_ROW = 16


def draw_row_adapter_index(key, part):
    key = jax.random.fold_in(key, 3)
    owner_key, local_key, mixing_key = jax.random.split(key, 3)
    positions = jnp.arange(ROWS, dtype=jnp.int32)
    half_rows = ROWS // 2
    heavy_owners = N_ROW // 8
    rank_of = jnp.where(positions < half_rows, positions // CAPO, heavy_owners + (positions - half_rows) % (N_ROW - heavy_owners))
    owner_perm = jax.random.permutation(owner_key, N_ROW).astype(jnp.int32)
    owner_of = owner_perm[rank_of]
    local_pick = jax.random.randint(local_key, (ROWS,), 0, ADP_DEV, dtype=jnp.int32)
    adapters = owner_of * ADP_DEV + local_pick
    shuffle = jax.random.permutation(mixing_key, ROWS)
    return adapters[shuffle].astype(jnp.int32)


def draw_cached_rotated_keys(key, part):
    key = jax.random.fold_in(key, 7)
    base_key = jax.random.fold_in(key, 0)
    target_shape = (ROWS, PREFIX, KEYVALUE_WIDTH)
    values = jnp.clip(jax.random.normal(base_key, target_shape, jnp.float32), -6.0, 6.0)
    return values.astype(jnp.bfloat16)


def level_of(own_key, shape, cuts, low, largest):
    factor_of = 1.0
    for axis_at, parts in cuts:
        steps = jax.random.uniform(jax.random.fold_in(jax.random.fold_in(own_key, 6), axis_at), (parts,), jnp.float32, low / len(cuts), largest / len(cuts))
        factor_of = factor_of * jnp.repeat(jnp.exp(steps), shape[axis_at] // parts).reshape((-1,) + (1,) * (len(shape) - 1 - axis_at))
    return factor_of


def scatter_about(key, dims, width, bound, cuts=(), held_as=jnp.bfloat16):
    array = width * jax.random.normal(key, dims, jnp.float32)
    if cuts:
        array = array * level_of(key, dims, cuts, -0.22, 0.18)
    return jnp.clip(array, -bound, bound).astype(held_as)


def setup_inputs(seed: int = 0, part: int = 0) -> dict:
    arg_keys = jax.random.split(jax.random.key(seed), 11)
    own_keys = jax.random.split(jax.random.fold_in(arg_keys[10], part), 11)
    tokens = scatter_about(own_keys[0], (ROWS, MODEL_DIMENSION), 1.0, 6.0, ((0, 16),))
    attention_norm_gain = jnp.clip(1.0 + 0.18 * jax.random.normal(arg_keys[1], (MODEL_DIMENSION,), jnp.float32), 0.1, 1.9)
    query_weight = scatter_about(arg_keys[2], (MODEL_DIMENSION, MODEL_DIMENSION), MODEL_DIMENSION ** -0.5, 0.0625, ((1, 16),))
    keyvalue_weight = scatter_about(arg_keys[3], (MODEL_DIMENSION, 2, KEYVALUE_WIDTH), MODEL_DIMENSION ** -0.5, 0.0625, ((2, 16),))
    adapter_down_weight = scatter_about(arg_keys[4], (ADAPTER_COUNT, 2 * ADAPTER_RANK, MODEL_DIMENSION), MODEL_DIMENSION ** -0.5, 0.0625, ((0, 16),))
    adapter_query_up = scatter_about(arg_keys[5], (ADAPTER_COUNT, ADAPTER_RANK, MODEL_DIMENSION), ADAPTER_RANK ** -0.5, 1.0, ((2, 16),))
    adapter_value_up = scatter_about(arg_keys[6], (ADAPTER_COUNT, ADAPTER_RANK, KEYVALUE_WIDTH), ADAPTER_RANK ** -0.5, 1.0, ((2, 16),))
    cached_rotated_keys = draw_cached_rotated_keys(jax.random.fold_in(jax.random.fold_in(arg_keys[10], part), 71), part)
    cached_value_rows = scatter_about(own_keys[8], (ROWS, PREFIX, KEYVALUE_WIDTH), 1.0, 6.0, ((0, 16),))
    row_adapter_index = draw_row_adapter_index(jax.random.fold_in(jax.random.fold_in(arg_keys[10], part), 71), part)
    return {"tokens": tokens, "attention_norm_gain": attention_norm_gain, "query_weight": query_weight, "keyvalue_weight": keyvalue_weight, "adapter_down_weight": adapter_down_weight, "adapter_query_up": adapter_query_up, "adapter_value_up": adapter_value_up, "cached_rotated_keys": cached_rotated_keys, "cached_value_rows": cached_value_rows, "row_adapter_index": row_adapter_index}


eps_value = 1e-05
adapter_scale = 2.0
rope_base = 500000.0

def rms_normed(tokens, attention_norm_gain):
    values = tokens.astype(jnp.float32)
    mean_square = lax.optimization_barrier(jnp.mean(values * values, axis=-1, keepdims=True))
    return (values * lax.rsqrt(mean_square + eps_value) * attention_norm_gain).astype(jnp.bfloat16)

def rotate(vectors, position):
    half_width = vectors.shape[-1] // 2
    fraction = jnp.arange(half_width, dtype=jnp.float32) / half_width
    angles = position * jnp.exp(-fraction * math.log(rope_base))
    cosine = jnp.cos(angles)
    sine_part = jnp.sin(angles)
    front_half = vectors[..., :half_width]
    back_half = vectors[..., half_width:]
    return jnp.concatenate([front_half * cosine - back_half * sine_part, back_half * cosine + front_half * sine_part], axis=-1)

def attend_block(inputs):
    query, keys_new, values_new, old_keys, old_values = inputs
    rows_here = query.shape[0]
    prefix_len = old_keys.shape[1]
    groups = HEADS // KV_HEADS
    grouped = query.astype(jnp.float32).reshape(rows_here, KV_HEADS, groups, HEAD_DIM)
    past_keys = old_keys.astype(jnp.float32).reshape(rows_here, prefix_len, KV_HEADS, HEAD_DIM)
    past_values = old_values.astype(jnp.float32).reshape(rows_here, prefix_len, KV_HEADS, HEAD_DIM)
    fresh_keys = keys_new.astype(jnp.float32).reshape(rows_here, KV_HEADS, HEAD_DIM)
    fresh_values = values_new.astype(jnp.float32).reshape(rows_here, KV_HEADS, 1, HEAD_DIM)
    scale = HEAD_DIM ** (-0.5)
    old_scores = jnp.einsum('rkgd,rpkd->rkgp', grouped, past_keys) * scale
    new_scores = jnp.einsum('rkgd,rkd->rkg', grouped, fresh_keys)[..., None] * scale
    scores = jnp.concatenate([old_scores, new_scores], axis=-1)
    peak = lax.optimization_barrier(jnp.max(scores, axis=-1, keepdims=True))
    expo = jnp.exp(scores - peak)
    weights = (expo / lax.optimization_barrier(jnp.sum(expo, axis=-1, keepdims=True))).astype(jnp.bfloat16).astype(jnp.float32)
    mixed = jnp.einsum('rkgp,rpkd->rkgd', weights[..., :prefix_len], past_values)
    mixed = mixed + weights[..., prefix_len:] * fresh_values
    return mixed.reshape(rows_here, HEADS * HEAD_DIM).astype(jnp.bfloat16)

def reference(tokens, attention_norm_gain, query_weight, keyvalue_weight, adapter_down_weight, adapter_query_up, adapter_value_up, cached_rotated_keys, cached_value_rows, row_adapter_index):
    normed = rms_normed(tokens, attention_norm_gain)
    row_total = normed.shape[0]
    base_query_output = jnp.dot(normed, query_weight, preferred_element_type=jnp.float32)
    base_k = jnp.dot(normed, keyvalue_weight[:, 0, :], preferred_element_type=jnp.float32)
    base_value_output = jnp.dot(normed, keyvalue_weight[:, 1, :], preferred_element_type=jnp.float32)

    def down_one(keyvalue_couple):
        return jnp.dot(adapter_down_weight[keyvalue_couple[1]], keyvalue_couple[0], preferred_element_type=jnp.float32)
    low = lax.map(down_one, (normed, row_adapter_index)).astype(jnp.bfloat16)

    def up_query(keyvalue_couple):
        return jnp.dot(keyvalue_couple[0][:ADAPTER_RANK], adapter_query_up[keyvalue_couple[1]], preferred_element_type=jnp.float32)

    def up_value(keyvalue_couple):
        return jnp.dot(keyvalue_couple[0][ADAPTER_RANK:], adapter_value_up[keyvalue_couple[1]], preferred_element_type=jnp.float32)
    query_correction = lax.map(up_query, (low, row_adapter_index))
    value_correction = lax.map(up_value, (low, row_adapter_index))
    query_before_rotation = (base_query_output + adapter_scale * query_correction).astype(jnp.bfloat16)
    key_pre = base_k.astype(jnp.bfloat16)
    incoming_values = (base_value_output + adapter_scale * value_correction).astype(jnp.bfloat16)
    position = float(cached_rotated_keys.shape[1])
    query = rotate(query_before_rotation.astype(jnp.float32).reshape(row_total, HEADS, HEAD_DIM), position).astype(jnp.bfloat16)
    new_keys = rotate(key_pre.astype(jnp.float32).reshape(row_total, KV_HEADS, HEAD_DIM), position).astype(jnp.bfloat16)
    new_keys = new_keys.reshape(row_total, KV_HEADS * HEAD_DIM)
    blocks = row_total // ROW_DEV
    prefix_len = cached_rotated_keys.shape[1]
    context = lax.map(attend_block, (query.reshape(blocks, ROW_DEV, HEADS, HEAD_DIM), new_keys.reshape(blocks, ROW_DEV, KV_HEADS * HEAD_DIM), incoming_values.reshape(blocks, ROW_DEV, KV_HEADS * HEAD_DIM), cached_rotated_keys.reshape(blocks, ROW_DEV, prefix_len, KV_HEADS * HEAD_DIM), cached_value_rows.reshape(blocks, ROW_DEV, prefix_len, KV_HEADS * HEAD_DIM)))
    context = context.reshape(row_total, HEADS * HEAD_DIM)
    return (context, new_keys, incoming_values)
```

```python
import math

import jax
import jax.numpy as jnp
from jax import lax
from jax.experimental import pallas as pl
from jax.experimental.pallas import tpu as pltpu
from jax.sharding import PartitionSpec as P

HEAD_DIM = 128
CAPO = 64
LANES = 128
MESH = pl.DeviceIdType.MESH

eps_value = 1e-05
adapter_scale = 2.0
rope_base = 500000.0

K_PIECES = 4
CHUNK_CHIPS = 4


def rotation_table(position):
    half_width = HEAD_DIM // 2
    fraction = jnp.arange(half_width, dtype=jnp.float32) / half_width
    angles = position * jnp.exp(-fraction * math.log(rope_base))
    cosine = jnp.cos(angles)
    sine_part = jnp.sin(angles)
    return jnp.stack(
        [jnp.concatenate([cosine, cosine]), jnp.concatenate([-sine_part, sine_part])]
    )


def row_codes(row_adapter_index, per_adapter_rows):
    owner = row_adapter_index // per_adapter_rows
    places = jnp.arange(owner.shape[0], dtype=jnp.int32)
    earlier = (owner[:, None] == owner[None, :]) & (places[None, :] < places[:, None])
    rank = jnp.sum(earlier.astype(jnp.int32), axis=1)
    code = row_adapter_index * CAPO + rank
    return jnp.broadcast_to(code[:, None], (owner.shape[0], LANES))


def kernel(
    n,
    adapters,
    own,
    tokens_ref,
    gain_ref,
    table_ref,
    code_ref,
    wq_hbm,
    down_hbm,
    wkv_hbm,
    uq_hbm,
    uv_hbm,
    keys_hbm,
    values_hbm,
    context_ref,
    new_keys_ref,
    new_values_ref,
    gathered,
    wq,
    side,
    uq,
    uv,
    keys,
    values,
    acc,
    acc_side,
    compact,
    low_slots,
    out_blocks,
    in_blocks,
    load_sem,
    ring_send,
    ring_recv,
    sib_send,
    sib_recv,
    low_send,
    low_recv,
    out_send,
    in_recv,
):
    group = lax.axis_index("grp")
    me = lax.axis_index("row")
    rows, width = tokens_ref.shape
    chips = n // 2
    far = chips // 2
    half = width // 2
    q_cols = wq.shape[1]
    k_cols = wkv_hbm.shape[0] // 2
    downs = down_hbm.shape[0]
    core = lax.rem(me, 2)
    chip = me // 2
    snake = chips == 8

    def to_position(c):
        if not snake:
            return c
        z, y = c // 2, lax.rem(c, 2)
        return z + y * (chips - 1 - 2 * z)

    def to_chip(p):
        if not snake:
            return p
        y = p // far
        return 2 * (p + y * (chips - 1 - 2 * p)) + y

    place = to_position(chip)

    def device_at(offset, other_core):
        c = to_chip(lax.rem(place + (offset + chips), chips))
        return 2 * c + (1 - core if other_core else core)

    neighbours = (device_at(1, False), device_at(-1, False))
    sibling = 2 * chip + 1 - core

    def slot_of(way, s):
        if s == 0:
            return 0
        if s == far:
            return chips - 1
        return 2 * s - 1 + way

    slot_offset = [0] * chips
    for s in range(1, far):
        slot_offset[slot_of(0, s)] = -s
        slot_offset[slot_of(1, s)] = s
    slot_offset[chips - 1] = far
    block_device = [
        device_at(slot_offset[b // 2], b % 2 == 1) for b in range(n)
    ]

    loads = [
        pltpu.make_async_copy(a, b, load_sem.at[i])
        for i, (a, b) in enumerate(
            [
                (wq_hbm, wq),
                (down_hbm, side.at[pl.ds(0, downs), :]),
                (wkv_hbm, side.at[pl.ds(downs, 2 * k_cols), :]),
                (uq_hbm, uq),
                (uv_hbm, uv),
                (keys_hbm, keys),
                (values_hbm, values),
            ]
        )
    ]
    for load in loads:
        load.start()

    barrier = pltpu.get_barrier_semaphore()

    @pl.loop(1, n)
    def _(d):
        pl.semaphore_signal(
            barrier, inc=1, device_id=(group, lax.rem(me + d, n)), device_id_type=MESH
        )

    tokens = tokens_ref[...].astype(jnp.float32)
    mean_square = jnp.sum(tokens * tokens, axis=1, keepdims=True) / width
    gathered[0:rows, :] = (tokens * lax.rsqrt(mean_square + eps_value) * gain_ref[...]).astype(
        jnp.bfloat16
    )
    compact[...] = jnp.zeros_like(compact)
    pl.semaphore_wait(barrier, n - 1)

    def reach(way, h):
        return far if way == h else far - 1

    def block(slot, other, h):
        start = (2 * slot + other) * rows
        return gathered.at[pl.ds(start, rows), pl.ds(h * half, half)]

    def ring(way, s, h):
        i = (way * far + s - 1) * 2 + h
        return pltpu.make_async_remote_copy(
            src_ref=block(slot_of(way, s - 1), 0, h),
            dst_ref=block(slot_of(way, s), 0, h),
            send_sem=ring_send.at[i],
            recv_sem=ring_recv.at[i],
            device_id=(group, neighbours[way]),
            device_id_type=MESH,
        )

    def across(way, s, h):
        i = (way * (far + 1) + s) * 2 + h
        return pltpu.make_async_remote_copy(
            src_ref=block(slot_of(way, s), 0, h),
            dst_ref=block(slot_of(way, s), 1, h),
            send_sem=sib_send.at[i],
            recv_sem=sib_recv.at[i],
            device_id=(group, sibling),
            device_id_type=MESH,
        )

    ring_steps = [
        (way, s, h)
        for s in range(1, far + 1)
        for h in range(2)
        for way in range(2)
        if s <= reach(way, h)
    ]
    across_steps = [(0, 0, 0), (0, 0, 1)] + ring_steps

    for way, s, h in ring_steps:
        if s == 1:
            ring(way, s, h).start()
    across(0, 0, 0).start()
    across(0, 0, 1).start()

    chunk_rows = CHUNK_CHIPS * 2 * rows
    chunks = chips // CHUNK_CHIPS
    depth = width // K_PIECES
    arrived = set()

    def wait_across(chunk):
        for step in across_steps:
            if step not in arrived and slot_of(*step[:2]) // CHUNK_CHIPS <= chunk:
                arrived.add(step)
                across(*step).wait_recv()

    def add_to(total, at, piece, value):
        if piece == 0:
            total[at, :] = value
        else:
            total[at, :] += value

    def side_piece(chunk, piece):
        at = pl.ds(chunk * chunk_rows, chunk_rows)
        span = pl.ds(piece * depth, depth)
        product = lax.dot_general(
            gathered[at, span],
            side[:, span],
            (((1,), (1,)), ((), ())),
            preferred_element_type=jnp.float32,
        )
        add_to(acc_side, at, piece, product)

    def query_piece(chunk, piece):
        at = pl.ds(chunk * chunk_rows, chunk_rows)
        span = pl.ds(piece * depth, depth)
        product = jnp.dot(gathered[at, span], wq[span, :], preferred_element_type=jnp.float32)
        add_to(acc, at, piece, product)

    shape = (chunk_rows, LANES)
    lane = lax.broadcasted_iota(jnp.int32, shape, 1)
    own_bits = own.bit_length() - 1

    def chunk_codes(chunk):
        first = chunk * CHUNK_CHIPS * 2
        code = jnp.concatenate(
            [
                code_ref[pl.ds(pl.multiple_of(block_device[b] * rows, rows), rows), :]
                for b in range(first, first + CHUNK_CHIPS * 2)
            ],
            axis=0,
        )
        adapter = code >> 6
        return adapter, adapter >> own_bits, code & (CAPO - 1)

    def pack_low(chunk):
        adapter, owner, rank = chunk_codes(chunk)
        at = pl.ds(chunk * chunk_rows, chunk_rows)
        low = jnp.zeros(shape, jnp.float32)
        for t in range(own // 2):
            local = me * own + 2 * t + (lane >> 6)
            low += jnp.where(adapter == local, acc_side[at, t * LANES : (t + 1) * LANES], 0.0)
        low = low + pltpu.roll(low, 64, 1)
        chosen = jnp.where((rank == lane) & (owner == me), 1.0, 0.0).astype(jnp.bfloat16)
        compact[...] += lax.dot_general(
            chosen,
            low.astype(jnp.bfloat16),
            (((0,), (0,)), ((), ())),
            preferred_element_type=jnp.float32,
        )

    todo = []

    def fill():
        if todo:
            todo.pop(0)()

    def queue(chunk):
        def first():
            wait_across(chunk)
            if chunk == 0:
                loads[0].wait()
                loads[1].wait()
                loads[2].wait()

        def make(piece):
            def run():
                if piece == 0:
                    first()
                side_piece(chunk, piece)
                query_piece(chunk, piece)
                if piece == K_PIECES - 1:
                    pack_low(chunk)

            return run

        todo.extend(make(piece) for piece in range(K_PIECES))

    queued = 0
    for s in range(1, far + 1):
        for h in range(2):
            for way in range(2):
                if s > reach(way, h):
                    continue
                ring(way, s, h).wait_recv()
                if s + 1 <= reach(way, h):
                    ring(way, s + 1, h).start()
                across(way, s, h).start()
            fill()
        while queued < chunks - 1 and (queued + 1) * CHUNK_CHIPS <= 2 * s + 1:
            queue(queued)
            queued += 1
    while todo:
        fill()
    last = chunks - 1
    wait_across(last)
    for piece in range(K_PIECES):
        side_piece(last, piece)
    pack_low(last)

    lane32 = lax.broadcasted_iota(jnp.int32, (CAPO // 2, LANES), 1)
    low_slots[me] = jnp.where(
        lane32 < 64, compact[0 : CAPO // 2, :], compact[CAPO // 2 : CAPO, :]
    ).astype(jnp.bfloat16)

    def low_copy(d):
        return pltpu.make_async_remote_copy(
            src_ref=low_slots.at[me],
            dst_ref=low_slots.at[me],
            send_sem=low_send.at[d],
            recv_sem=low_recv.at[me],
            device_id=(group, lax.rem(me + d, n)),
            device_id_type=MESH,
        )

    def low_arrival(d):
        source = lax.rem(me + d, n)
        return pltpu.make_async_remote_copy(
            src_ref=low_slots.at[source],
            dst_ref=low_slots.at[source],
            send_sem=low_send.at[d],
            recv_sem=low_recv.at[source],
            device_id=(group, source),
            device_id_type=MESH,
        )

    @pl.loop(1, n)
    def _(d):
        low_copy(d).start()

    for piece in range(K_PIECES):
        query_piece(last, piece)

    @pl.loop(1, n)
    def _(d):
        low_arrival(d).wait_recv()

    loads[3].wait()
    loads[4].wait()

    def out_copy(b):
        return pltpu.make_async_remote_copy(
            src_ref=out_blocks.at[b],
            dst_ref=in_blocks.at[me],
            send_sem=out_send.at[b],
            recv_sem=in_recv.at[me],
            device_id=(group, block_device[b]),
            device_id_type=MESH,
        )

    def in_arrival(b):
        source = block_device[b]
        return pltpu.make_async_remote_copy(
            src_ref=out_blocks.at[b],
            dst_ref=in_blocks.at[source],
            send_sem=out_send.at[b],
            recv_sem=in_recv.at[source],
            device_id=(group, source),
            device_id_type=MESH,
        )

    all_low = low_slots[...].reshape(n * (CAPO // 2), LANES)
    for chunk in range(chunks):
        at = pl.ds(chunk * chunk_rows, chunk_rows)
        adapter, owner, rank = chunk_codes(chunk)
        target = owner * (CAPO // 2) + (rank & (CAPO // 2 - 1))
        expand = jnp.concatenate(
            [
                jnp.where(target == lane + t * LANES, 1.0, 0.0).astype(jnp.bfloat16)
                for t in range(n * (CAPO // 2) // LANES)
            ],
            axis=1,
        )
        low = jnp.dot(expand, all_low, preferred_element_type=jnp.float32)
        low = jnp.where((rank >> 5) == (lane >> 6), low, 0.0) * adapter_scale
        low = low + pltpu.roll(low, 64, 1)
        turned = pltpu.roll(low, 32, 1)
        even = ((lane >> 5) & 1) == 0
        low_q = jnp.where(even, low, turned)
        low_v = jnp.where(even, turned, low)
        spread_q, spread_v = [], []
        for t in range(adapters * 32 // LANES):
            hit = adapter == 4 * t + (lane >> 5)
            spread_q.append(jnp.where(hit, low_q, 0.0).astype(jnp.bfloat16))
            spread_v.append(jnp.where(hit, low_v, 0.0).astype(jnp.bfloat16))
        query = acc[at, :] + jnp.dot(
            jnp.concatenate(spread_q, axis=1), uq[...], preferred_element_type=jnp.float32
        )
        shift = jnp.dot(
            jnp.concatenate(spread_v, axis=1), uv[...], preferred_element_type=jnp.float32
        )
        pair = acc_side[at, downs : downs + 2 * k_cols]
        pair = jnp.concatenate([pair[:, :k_cols], pair[:, k_cols:] + shift], axis=1)
        query = query.astype(jnp.bfloat16)
        pair = pair.astype(jnp.bfloat16)
        for i in range(CHUNK_CHIPS * 2):
            b = chunk * CHUNK_CHIPS * 2 + i
            out_blocks[b, :, 0:q_cols] = query[i * rows : (i + 1) * rows, :]
            out_blocks[b, :, q_cols : q_cols + 2 * k_cols] = pair[i * rows : (i + 1) * rows, :]
            if b > 0:
                out_copy(b).start()
        if chunk == 0:
            in_blocks[me] = out_blocks[0]

    loads[5].wait()
    loads[6].wait()
    for b in range(1, n):
        in_arrival(b).wait_recv()

    heads = n * q_cols // HEAD_DIM
    kv_heads = n * k_cols // HEAD_DIM
    per_kv = heads // kv_heads
    sharers = n // kv_heads
    cached = keys.shape[0]
    prefix = cached // rows
    cosine = table_ref[0:1, :]
    sine = table_ref[1:2, :]

    def rotate(vectors):
        vectors = vectors.astype(jnp.float32)
        return (vectors * cosine + pltpu.roll(vectors, HEAD_DIM // 2, 1) * sine).astype(
            jnp.bfloat16
        )

    stacked = per_kv * rows
    row_of = lax.broadcasted_iota(jnp.int32, (stacked, cached), 0) & (rows - 1)
    column = lax.broadcasted_iota(jnp.int32, (stacked, cached), 1)
    same_row = (column >= row_of * prefix) & (column < (row_of + 1) * prefix)
    scale = HEAD_DIM ** (-0.5)
    for k in range(kv_heads):
        span = pl.ds(k * HEAD_DIM, HEAD_DIM)
        pieces = [in_blocks[k * sharers + i] for i in range(sharers)]
        query = jnp.concatenate(
            [
                piece[:, j * HEAD_DIM : (j + 1) * HEAD_DIM]
                for piece in pieces
                for j in range(q_cols // HEAD_DIM)
            ],
            axis=0,
        )
        key_new = jnp.concatenate([p[:, q_cols : q_cols + k_cols] for p in pieces], axis=1)
        value_new = jnp.concatenate(
            [p[:, q_cols + k_cols : q_cols + 2 * k_cols] for p in pieces], axis=1
        )
        query = rotate(query)
        key_new = rotate(key_new)
        new_keys_ref[:, span] = key_new
        new_values_ref[:, span] = value_new
        old = lax.dot_general(
            query, keys[:, span], (((1,), (1,)), ((), ())), preferred_element_type=jnp.float32
        )
        old = jnp.where(same_row, old * scale, -1e30)
        key_all = jnp.concatenate([key_new.astype(jnp.float32)] * per_kv, axis=0)
        value_all = jnp.concatenate([value_new.astype(jnp.float32)] * per_kv, axis=0)
        fresh = jnp.sum(query.astype(jnp.float32) * key_all, axis=1, keepdims=True) * scale
        peak = jnp.maximum(jnp.max(old, axis=1, keepdims=True), fresh)
        expo = jnp.exp(old - peak)
        expo_new = jnp.exp(fresh - peak)
        share = 1.0 / (jnp.sum(expo, axis=1, keepdims=True) + expo_new)
        weights = (expo * share).astype(jnp.bfloat16)
        weight_new = (expo_new * share).astype(jnp.bfloat16).astype(jnp.float32)
        mixed = jnp.dot(weights, values[:, span], preferred_element_type=jnp.float32)
        mixed = (mixed + weight_new * value_all).astype(jnp.bfloat16)
        for j in range(per_kv):
            at = (k * per_kv + j) * HEAD_DIM
            context_ref[:, at : at + HEAD_DIM] = mixed[j * rows : (j + 1) * rows, :]

    for step in ring_steps:
        ring(*step).wait_send()
    for step in across_steps:
        across(*step).wait_send()

    @pl.loop(1, n)
    def _(d):
        low_copy(d).wait_send()

    for b in range(1, n):
        out_copy(b).wait_send()


def shards(
    tokens,
    attention_norm_gain,
    query_weight,
    keyvalue_weight,
    adapter_down_weight,
    adapter_query_up,
    adapter_value_up,
    cached_rotated_keys,
    cached_value_rows,
    row_adapter_index,
):
    n = lax.axis_size("row")
    rows, width = tokens.shape
    total = row_adapter_index.shape[0]
    own, ranks, _ = adapter_down_weight.shape
    adapters, rank, q_cols = adapter_query_up.shape
    k_cols = keyvalue_weight.shape[2]
    prefix, kv_width = cached_rotated_keys.shape[1:]
    table = rotation_table(float(prefix))
    code = row_codes(row_adapter_index, own)
    wkv = jnp.transpose(keyvalue_weight, (1, 2, 0)).reshape(2 * k_cols, width)
    down = adapter_down_weight.reshape(own * ranks, width)
    uq = adapter_query_up.reshape(adapters * rank, q_cols)
    uv = adapter_value_up.reshape(adapters * rank, k_cols)
    keys = cached_rotated_keys.reshape(rows * prefix, kv_width)
    values = cached_value_rows.reshape(rows * prefix, kv_width)
    side_rows = own * ranks + 2 * k_cols
    hbm = [query_weight, down, wkv, uq, uv, keys, values]
    far = n // 4
    bf16, f32 = jnp.bfloat16, jnp.float32
    dma = pltpu.SemaphoreType.DMA

    def body(*refs):
        kernel(n, adapters, own, *refs)

    vmem = pl.BlockSpec(memory_space=pltpu.VMEM)
    return pl.pallas_call(
        body,
        out_shape=(
            jax.ShapeDtypeStruct((rows, n * q_cols), bf16),
            jax.ShapeDtypeStruct((rows, n * k_cols), bf16),
            jax.ShapeDtypeStruct((rows, n * k_cols), bf16),
        ),
        in_specs=[vmem] * 4 + [pl.BlockSpec(memory_space=pl.ANY)] * len(hbm),
        out_specs=(vmem, vmem, vmem),
        scratch_shapes=[pltpu.VMEM((total, width), bf16)]
        + [pltpu.VMEM(query_weight.shape, bf16), pltpu.VMEM((side_rows, width), bf16)]
        + [pltpu.VMEM(a.shape, bf16) for a in hbm[3:]]
        + [
            pltpu.VMEM((total, q_cols), f32),
            pltpu.VMEM((total, side_rows), f32),
            pltpu.VMEM((LANES, LANES), f32),
            pltpu.VMEM((n, CAPO // 2, LANES), bf16),
            pltpu.VMEM((n, rows, q_cols + 2 * k_cols), bf16),
            pltpu.VMEM((n, rows, q_cols + 2 * k_cols), bf16),
            dma((len(hbm),)),
            dma((4 * far,)),
            dma((4 * far,)),
            dma((4 * (far + 1),)),
            dma((4 * (far + 1),)),
            dma((n,)),
            dma((n,)),
            dma((n,)),
            dma((n,)),
        ],
        compiler_params=pltpu.CompilerParams(
            collective_id=0, has_side_effects=True, vmem_limit_bytes=56 * 1024 * 1024
        ),
    )(tokens, attention_norm_gain.reshape(1, width), table, code, *hbm)


def solution(mesh):
    return jax.shard_map(
        shards,
        mesh=mesh,
        in_specs=(
            P(("grp", "row"), None),
            P(),
            P(None, "row"),
            P(None, None, "row"),
            P("row", None, None),
            P(None, None, "row"),
            P(None, None, "row"),
            P(("grp", "row"), None, None),
            P(("grp", "row"), None, None),
            P("grp"),
        ),
        out_specs=(P(("grp", "row"), None), P(("grp", "row"), None), P(("grp", "row"), None)),
        check_vma=False,
    )
```

```python
import math

import jax
import jax.numpy as jnp
import numpy as np
from jax import lax
from jax.experimental import pallas as pl
from jax.experimental.pallas import tpu as pltpu
from jax.sharding import PartitionSpec as P

HEAD_DIM = 128
CAPO = 64
LANES = 128
MESH = pl.DeviceIdType.MESH

eps_value = 1e-05
adapter_scale = 2.0
rope_base = 500000.0

K_PIECES = 4
PARTS = 4
CHUNK_CHIPS = 4


def rotation_table(position):
    half_width = HEAD_DIM // 2
    fraction = np.arange(half_width, dtype=np.float32) / np.float32(half_width)
    angles = np.float32(position) * np.exp(-fraction * np.float32(math.log(rope_base)))
    cosine = np.cos(angles)
    sine_part = np.sin(angles)
    rows = [np.concatenate([cosine, cosine]), np.concatenate([-sine_part, sine_part])]
    return jnp.asarray(np.stack(rows).astype(np.float32))


def write_codes(index_ref, code_ref, own_bits):
    square = (LANES, LANES)
    lane = lax.broadcasted_iota(jnp.int32, square, 1)
    row = lax.broadcasted_iota(jnp.int32, square, 0)
    groups = index_ref.shape[0]
    along = [
        jnp.broadcast_to(index_ref[g : g + 1, :].astype(jnp.float32), square) for g in range(groups)
    ]
    for g in range(groups):
        adapter = along[g].T.astype(jnp.int32)
        owner = adapter >> own_bits
        count = jnp.zeros(square, jnp.float32)
        for other in range(g + 1):
            same = (along[other].astype(jnp.int32) >> own_bits) == owner
            if other == g:
                same = same & (lane < row)
            count += jnp.where(same, 1.0, 0.0)
        rank = jnp.sum(count, axis=1, keepdims=True).astype(jnp.int32)
        code_ref[g * LANES : (g + 1) * LANES, :] = adapter * CAPO + rank


def kernel(
    n,
    adapters,
    own,
    tokens_ref,
    gain_ref,
    table_ref,
    index_ref,
    wq_hbm,
    down_hbm,
    wkv_hbm,
    uq_hbm,
    uv_hbm,
    keys_hbm,
    values_hbm,
    context_ref,
    new_keys_ref,
    new_values_ref,
    code_ref,
    gathered,
    wq,
    side,
    uq,
    uv,
    keys,
    values,
    acc,
    acc_side,
    compact,
    low_slots,
    out_blocks,
    in_blocks,
    load_sem,
    ring_send,
    ring_recv,
    sib_send,
    sib_recv,
    low_send,
    low_recv,
    out_send,
    in_recv,
):
    group = lax.axis_index("grp")
    me = lax.axis_index("row")
    rows, width = tokens_ref.shape
    chips = n // 2
    far = chips // 2
    part = width // PARTS
    q_cols = wq.shape[1]
    k_cols = wkv_hbm.shape[0] // 2
    downs = down_hbm.shape[0]
    core = lax.rem(me, 2)
    chip = me // 2
    snake = chips == 8

    def to_position(c):
        if not snake:
            return c
        z, y = c // 2, lax.rem(c, 2)
        return z + y * (chips - 1 - 2 * z)

    def to_chip(p):
        if not snake:
            return p
        y = p // far
        return 2 * (p + y * (chips - 1 - 2 * p)) + y

    place = to_position(chip)

    def device_at(offset, other_core):
        c = to_chip(lax.rem(place + (offset + chips), chips))
        return 2 * c + (1 - core if other_core else core)

    neighbours = (device_at(1, False), device_at(-1, False))
    sibling = 2 * chip + 1 - core

    def slot_of(way, s):
        if s == 0:
            return 0
        if s == far:
            return chips - 1
        return 2 * s - 1 + way

    slot_offset = [0] * chips
    for s in range(1, far):
        slot_offset[slot_of(0, s)] = -s
        slot_offset[slot_of(1, s)] = s
    slot_offset[chips - 1] = far
    block_device = [
        device_at(slot_offset[b // 2], b % 2 == 1) for b in range(n)
    ]

    loads = [
        pltpu.make_async_copy(a, b, load_sem.at[i])
        for i, (a, b) in enumerate(
            [
                (wq_hbm, wq),
                (down_hbm, side.at[pl.ds(0, downs), :]),
                (wkv_hbm, side.at[pl.ds(downs, 2 * k_cols), :]),
                (uq_hbm, uq),
                (uv_hbm, uv),
                (keys_hbm, keys),
                (values_hbm, values),
            ]
        )
    ]
    for load in loads:
        load.start()

    barrier = pltpu.get_barrier_semaphore()

    @pl.loop(1, n)
    def _(d):
        pl.semaphore_signal(
            barrier, inc=1, device_id=(group, lax.rem(me + d, n)), device_id_type=MESH
        )

    tokens = tokens_ref[...].astype(jnp.float32)
    mean_square = jnp.sum(tokens * tokens, axis=1, keepdims=True) / width
    gathered[0:rows, :] = (tokens * lax.rsqrt(mean_square + eps_value) * gain_ref[...]).astype(
        jnp.bfloat16
    )
    compact[...] = jnp.zeros_like(compact)
    pl.semaphore_wait(barrier, n - 1)

    def reach(way, h):
        return far if way == h // (PARTS // 2) else far - 1

    def block(slot, other, h):
        start = (2 * slot + other) * rows
        return gathered.at[pl.ds(start, rows), pl.ds(h * part, part)]

    def ring(way, s, h):
        i = (way * far + s - 1) * PARTS + h
        return pltpu.make_async_remote_copy(
            src_ref=block(slot_of(way, s - 1), 0, h),
            dst_ref=block(slot_of(way, s), 0, h),
            send_sem=ring_send.at[i],
            recv_sem=ring_recv.at[i],
            device_id=(group, neighbours[way]),
            device_id_type=MESH,
        )

    def across(way, s, h):
        i = (way * (far + 1) + s) * PARTS + h
        return pltpu.make_async_remote_copy(
            src_ref=block(slot_of(way, s), 0, h),
            dst_ref=block(slot_of(way, s), 1, h),
            send_sem=sib_send.at[i],
            recv_sem=sib_recv.at[i],
            device_id=(group, sibling),
            device_id_type=MESH,
        )

    ring_steps = [
        (way, s, h)
        for s in range(1, far + 1)
        for h in range(PARTS)
        for way in range(2)
        if s <= reach(way, h)
    ]
    across_steps = [(0, 0, h) for h in range(PARTS)] + ring_steps

    for way, s, h in ring_steps:
        if s == 1:
            ring(way, s, h).start()
    for h in range(PARTS):
        across(0, 0, h).start()

    own_bits = own.bit_length() - 1
    write_codes(index_ref, code_ref, own_bits)
    chunk_rows = CHUNK_CHIPS * 2 * rows
    chunks = chips // CHUNK_CHIPS
    depth = width // K_PIECES
    arrived = set()

    def wait_across(chunk):
        for step in across_steps:
            if step not in arrived and slot_of(*step[:2]) // CHUNK_CHIPS <= chunk:
                arrived.add(step)
                across(*step).wait_recv()

    def add_to(total, at, piece, value):
        if piece == 0:
            total[at, :] = value
        else:
            total[at, :] += value

    def side_piece(chunk, piece):
        at = pl.ds(chunk * chunk_rows, chunk_rows)
        span = pl.ds(piece * depth, depth)
        product = lax.dot_general(
            gathered[at, span],
            side[:, span],
            (((1,), (1,)), ((), ())),
            preferred_element_type=jnp.float32,
        )
        add_to(acc_side, at, piece, product)

    def query_piece(chunk, piece):
        at = pl.ds(chunk * chunk_rows, chunk_rows)
        span = pl.ds(piece * depth, depth)
        product = jnp.dot(gathered[at, span], wq[span, :], preferred_element_type=jnp.float32)
        add_to(acc, at, piece, product)

    shape = (chunk_rows, LANES)
    lane = lax.broadcasted_iota(jnp.int32, shape, 1)

    def chunk_codes(chunk):
        first = chunk * CHUNK_CHIPS * 2
        code = jnp.concatenate(
            [
                code_ref[pl.ds(pl.multiple_of(block_device[b] * rows, rows), rows), :]
                for b in range(first, first + CHUNK_CHIPS * 2)
            ],
            axis=0,
        )
        adapter = code >> 6
        return adapter, adapter >> own_bits, code & (CAPO - 1)

    def pack_low(chunk):
        adapter, owner, rank = chunk_codes(chunk)
        at = pl.ds(chunk * chunk_rows, chunk_rows)
        low = jnp.zeros(shape, jnp.float32)
        for t in range(own // 2):
            local = me * own + 2 * t + (lane >> 6)
            low += jnp.where(adapter == local, acc_side[at, t * LANES : (t + 1) * LANES], 0.0)
        low = low + pltpu.roll(low, 64, 1)
        chosen = jnp.where((rank == lane) & (owner == me), 1.0, 0.0).astype(jnp.bfloat16)
        compact[...] += lax.dot_general(
            chosen,
            low.astype(jnp.bfloat16),
            (((0,), (0,)), ((), ())),
            preferred_element_type=jnp.float32,
        )

    todo = []

    def fill():
        if todo:
            todo.pop(0)()

    def queue(chunk):
        def first():
            wait_across(chunk)
            if chunk == 0:
                loads[0].wait()
                loads[1].wait()
                loads[2].wait()

        def make(piece):
            def run():
                if piece == 0:
                    first()
                side_piece(chunk, piece)
                query_piece(chunk, piece)
                if piece == K_PIECES - 1:
                    pack_low(chunk)

            return run

        todo.extend(make(piece) for piece in range(K_PIECES))

    queued = 0
    for s in range(1, far + 1):
        for h in range(PARTS):
            for way in range(2):
                if s > reach(way, h):
                    continue
                ring(way, s, h).wait_recv()
                if s + 1 <= reach(way, h):
                    ring(way, s + 1, h).start()
                across(way, s, h).start()
            fill()
        while queued < chunks - 1 and (queued + 1) * CHUNK_CHIPS <= 2 * s + 1:
            queue(queued)
            queued += 1
    while todo:
        fill()
    last = chunks - 1
    wait_across(last)
    for piece in range(K_PIECES):
        side_piece(last, piece)
    pack_low(last)

    lane32 = lax.broadcasted_iota(jnp.int32, (CAPO // 2, LANES), 1)
    low_slots[me] = jnp.where(
        lane32 < 64, compact[0 : CAPO // 2, :], compact[CAPO // 2 : CAPO, :]
    ).astype(jnp.bfloat16)

    def low_copy(d):
        return pltpu.make_async_remote_copy(
            src_ref=low_slots.at[me],
            dst_ref=low_slots.at[me],
            send_sem=low_send.at[d],
            recv_sem=low_recv.at[me],
            device_id=(group, lax.rem(me + d, n)),
            device_id_type=MESH,
        )

    def low_arrival(d):
        source = lax.rem(me + d, n)
        return pltpu.make_async_remote_copy(
            src_ref=low_slots.at[source],
            dst_ref=low_slots.at[source],
            send_sem=low_send.at[d],
            recv_sem=low_recv.at[source],
            device_id=(group, source),
            device_id_type=MESH,
        )

    @pl.loop(1, n)
    def _(d):
        low_copy(d).start()

    for piece in range(K_PIECES):
        query_piece(last, piece)

    @pl.loop(1, n)
    def _(d):
        low_arrival(d).wait_recv()

    loads[3].wait()
    loads[4].wait()

    def out_copy(b):
        return pltpu.make_async_remote_copy(
            src_ref=out_blocks.at[b],
            dst_ref=in_blocks.at[me],
            send_sem=out_send.at[b],
            recv_sem=in_recv.at[me],
            device_id=(group, block_device[b]),
            device_id_type=MESH,
        )

    def in_arrival(b):
        source = block_device[b]
        return pltpu.make_async_remote_copy(
            src_ref=out_blocks.at[b],
            dst_ref=in_blocks.at[source],
            send_sem=out_send.at[b],
            recv_sem=in_recv.at[source],
            device_id=(group, source),
            device_id_type=MESH,
        )

    all_low = low_slots[...].reshape(n * (CAPO // 2), LANES)
    for chunk in range(chunks):
        at = pl.ds(chunk * chunk_rows, chunk_rows)
        adapter, owner, rank = chunk_codes(chunk)
        target = owner * (CAPO // 2) + (rank & (CAPO // 2 - 1))
        expand = jnp.concatenate(
            [
                jnp.where(target == lane + t * LANES, 1.0, 0.0).astype(jnp.bfloat16)
                for t in range(n * (CAPO // 2) // LANES)
            ],
            axis=1,
        )
        low = jnp.dot(expand, all_low, preferred_element_type=jnp.float32)
        low = jnp.where((rank >> 5) == (lane >> 6), low, 0.0) * adapter_scale
        low = low + pltpu.roll(low, 64, 1)
        turned = pltpu.roll(low, 32, 1)
        even = ((lane >> 5) & 1) == 0
        low_q = jnp.where(even, low, turned)
        low_v = jnp.where(even, turned, low)
        spread_q, spread_v = [], []
        for t in range(adapters * 32 // LANES):
            hit = adapter == 4 * t + (lane >> 5)
            spread_q.append(jnp.where(hit, low_q, 0.0).astype(jnp.bfloat16))
            spread_v.append(jnp.where(hit, low_v, 0.0).astype(jnp.bfloat16))
        query = acc[at, :] + jnp.dot(
            jnp.concatenate(spread_q, axis=1), uq[...], preferred_element_type=jnp.float32
        )
        shift = jnp.dot(
            jnp.concatenate(spread_v, axis=1), uv[...], preferred_element_type=jnp.float32
        )
        pair = acc_side[at, downs : downs + 2 * k_cols]
        pair = jnp.concatenate([pair[:, :k_cols], pair[:, k_cols:] + shift], axis=1)
        query = query.astype(jnp.bfloat16)
        pair = pair.astype(jnp.bfloat16)
        for i in range(CHUNK_CHIPS * 2):
            b = chunk * CHUNK_CHIPS * 2 + i
            out_blocks[b, :, 0:q_cols] = query[i * rows : (i + 1) * rows, :]
            out_blocks[b, :, q_cols : q_cols + 2 * k_cols] = pair[i * rows : (i + 1) * rows, :]
            if b > 0:
                out_copy(b).start()
        if chunk == 0:
            in_blocks[me] = out_blocks[0]

    loads[5].wait()
    loads[6].wait()
    heads = n * q_cols // HEAD_DIM
    kv_heads = n * k_cols // HEAD_DIM
    per_kv = heads // kv_heads
    sharers = n // kv_heads
    cached = keys.shape[0]
    prefix = cached // rows
    cosine = table_ref[0:1, :]
    sine = table_ref[1:2, :]

    def rotate(vectors):
        vectors = vectors.astype(jnp.float32)
        return (vectors * cosine + pltpu.roll(vectors, HEAD_DIM // 2, 1) * sine).astype(
            jnp.bfloat16
        )

    stacked = per_kv * rows
    row_of = lax.broadcasted_iota(jnp.int32, (stacked, cached), 0) & (rows - 1)
    column = lax.broadcasted_iota(jnp.int32, (stacked, cached), 1)
    same_row = (column >= row_of * prefix) & (column < (row_of + 1) * prefix)
    scale = HEAD_DIM ** (-0.5)
    by_chip = sharers == 2
    if not by_chip:
        for b in range(1, n):
            in_arrival(b).wait_recv()
    order = range(chips)
    for turn in range(kv_heads):
        if by_chip:
            slot = order[turn]
            k = block_device[2 * slot] // 2
            for b in (2 * slot, 2 * slot + 1):
                if b > 0:
                    in_arrival(b).wait_recv()
        else:
            k = turn
        span = pl.ds(pl.multiple_of(k * HEAD_DIM, HEAD_DIM), HEAD_DIM)
        pieces = [in_blocks[k * sharers + i] for i in range(sharers)]
        query = jnp.concatenate(
            [
                piece[:, j * HEAD_DIM : (j + 1) * HEAD_DIM]
                for piece in pieces
                for j in range(q_cols // HEAD_DIM)
            ],
            axis=0,
        )
        key_new = jnp.concatenate([p[:, q_cols : q_cols + k_cols] for p in pieces], axis=1)
        value_new = jnp.concatenate(
            [p[:, q_cols + k_cols : q_cols + 2 * k_cols] for p in pieces], axis=1
        )
        query = rotate(query)
        key_new = rotate(key_new)
        new_keys_ref[:, span] = key_new
        new_values_ref[:, span] = value_new
        old = lax.dot_general(
            query, keys[:, span], (((1,), (1,)), ((), ())), preferred_element_type=jnp.float32
        )
        old = jnp.where(same_row, old * scale, -1e30)
        key_all = jnp.concatenate([key_new.astype(jnp.float32)] * per_kv, axis=0)
        value_all = jnp.concatenate([value_new.astype(jnp.float32)] * per_kv, axis=0)
        fresh = jnp.sum(query.astype(jnp.float32) * key_all, axis=1, keepdims=True) * scale
        peak = jnp.maximum(jnp.max(old, axis=1, keepdims=True), fresh)
        expo = jnp.exp(old - peak)
        expo_new = jnp.exp(fresh - peak)
        share = 1.0 / (jnp.sum(expo, axis=1, keepdims=True) + expo_new)
        weights = (expo * share).astype(jnp.bfloat16)
        weight_new = (expo_new * share).astype(jnp.bfloat16).astype(jnp.float32)
        mixed = jnp.dot(weights, values[:, span], preferred_element_type=jnp.float32)
        mixed = (mixed + weight_new * value_all).astype(jnp.bfloat16)
        for j in range(per_kv):
            at = pl.multiple_of((k * per_kv + j) * HEAD_DIM, HEAD_DIM)
            context_ref[:, pl.ds(at, HEAD_DIM)] = mixed[j * rows : (j + 1) * rows, :]

    for step in ring_steps:
        ring(*step).wait_send()
    for step in across_steps:
        across(*step).wait_send()

    @pl.loop(1, n)
    def _(d):
        low_copy(d).wait_send()

    for b in range(1, n):
        out_copy(b).wait_send()


def hand_over(a, b, c, a_out, b_out, c_out):
    a_out[...] = a[...]
    b_out[...] = b[...]
    c_out[...] = c[...]


def shards(
    tokens,
    attention_norm_gain,
    query_weight,
    keyvalue_weight,
    adapter_down_weight,
    adapter_query_up,
    adapter_value_up,
    cached_rotated_keys,
    cached_value_rows,
    row_adapter_index,
):
    n = lax.axis_size("row")
    rows, width = tokens.shape
    total = row_adapter_index.shape[0]
    own, ranks, _ = adapter_down_weight.shape
    adapters, rank, q_cols = adapter_query_up.shape
    k_cols = keyvalue_weight.shape[2]
    prefix, kv_width = cached_rotated_keys.shape[1:]
    table = rotation_table(float(prefix))
    index = row_adapter_index.reshape(total // LANES, LANES)
    wkv = jnp.transpose(keyvalue_weight, (1, 2, 0)).reshape(2 * k_cols, width)
    down = adapter_down_weight.reshape(own * ranks, width)
    uq = adapter_query_up.reshape(adapters * rank, q_cols)
    uv = adapter_value_up.reshape(adapters * rank, k_cols)
    keys = cached_rotated_keys.reshape(rows * prefix, kv_width)
    values = cached_value_rows.reshape(rows * prefix, kv_width)
    side_rows = own * ranks + 2 * k_cols
    hbm = [query_weight, down, wkv, uq, uv, keys, values]
    far = n // 4
    bf16, f32 = jnp.bfloat16, jnp.float32
    dma = pltpu.SemaphoreType.DMA

    def body(*refs):
        kernel(n, adapters, own, *refs)

    vmem = pl.BlockSpec(memory_space=pltpu.VMEM)
    results = pl.pallas_call(
        body,
        out_shape=(
            jax.ShapeDtypeStruct((rows, n * q_cols), bf16),
            jax.ShapeDtypeStruct((rows, n * k_cols), bf16),
            jax.ShapeDtypeStruct((rows, n * k_cols), bf16),
        ),
        in_specs=[vmem] * 4 + [pl.BlockSpec(memory_space=pl.ANY)] * len(hbm),
        out_specs=(vmem, vmem, vmem),
        scratch_shapes=[pltpu.VMEM((total, LANES), jnp.int32), pltpu.VMEM((total, width), bf16)]
        + [pltpu.VMEM(query_weight.shape, bf16), pltpu.VMEM((side_rows, width), bf16)]
        + [pltpu.VMEM(a.shape, bf16) for a in hbm[3:]]
        + [
            pltpu.VMEM((total, q_cols), f32),
            pltpu.VMEM((total, side_rows), f32),
            pltpu.VMEM((LANES, LANES), f32),
            pltpu.VMEM((n, CAPO // 2, LANES), bf16),
            pltpu.VMEM((n, rows, q_cols + 2 * k_cols), bf16),
            pltpu.VMEM((n, rows, q_cols + 2 * k_cols), bf16),
            dma((len(hbm),)),
            dma((2 * PARTS * far,)),
            dma((2 * PARTS * far,)),
            dma((2 * PARTS * (far + 1),)),
            dma((2 * PARTS * (far + 1),)),
            dma((n,)),
            dma((n,)),
            dma((n,)),
            dma((n,)),
        ],
        compiler_params=pltpu.CompilerParams(
            collective_id=0, has_side_effects=True, vmem_limit_bytes=56 * 1024 * 1024
        ),
    )(tokens, attention_norm_gain.reshape(1, width), table, index, *hbm)
    return pl.pallas_call(
        hand_over,
        out_shape=tuple(jax.ShapeDtypeStruct(a.shape, a.dtype) for a in results),
        in_specs=[vmem] * 3,
        out_specs=(vmem,) * 3,
    )(*results)


def solution(mesh):
    return jax.shard_map(
        shards,
        mesh=mesh,
        in_specs=(
            P(("grp", "row"), None),
            P(),
            P(None, "row"),
            P(None, None, "row"),
            P("row", None, None),
            P(None, None, "row"),
            P(None, None, "row"),
            P(("grp", "row"), None, None),
            P(("grp", "row"), None, None),
            P("grp"),
        ),
        out_specs=(P(("grp", "row"), None), P(("grp", "row"), None), P(("grp", "row"), None)),
        check_vma=False,
    )
```
